32 devices in a mesh: gx: 4 (over x, core), gy: 8 (over z, y).
Axes of the slice: x: 2, y: 2, z: 4, core: 2. Of those that a mesh axis runs over, the one named last changes fastest.
Arguments:
- velocity_section: float32 [3, 64, 64, 1024], P(None, 'gx', None, 'gy')
- point_owner: int32 [4, 240], P('gx'), may hold values from 0 to 7
- point_cell: int32 [4, 3, 240], P('gx'), may hold values from 0 to 127, as said below
- blade_coef: float32 [4, 240], P('gx'), may hold values from 0.5 to 2
- recycle_map: int32 [8], replicated, may hold values from 0 to 7, as said below
Outputs:
- rate: float32 [3, 64, 64, 1024], P(None, 'gx', None, 'gy')
- spread: float32 [3, 64, 64, 1024], P(None, 'gx', None, 'gy')
- point_force: float32 [4, 3, 240], P('gx')
The draws below stay inside these ranges and needn't reach their ends.
Inputs may be any that keep to these rules, and one draw needn't show every extreme that they name: `point_cell`: row 0 is below 16, row 1 below 128, row 2 below 64. `recycle_map`: a permutation of the spanwise blocks.
All inputs are finite; a program needn't handle non-finite values.
Results may differ from the reference program's by a relative error of at most 0.0022.
Values sent between devices are 32-bit elements; how exact they have to be, the bound alone decides.
A program may use at most 192 MiB of HBM per device.

```python
import math
import jax
import jax.numpy as jnp
import numpy as np
from jax import lax

CX = 16
CY = 128
NZ = 64
TURB_COL = 2
BLADES = 3
BLADE_PTS = 40
ROTOR_RADIUS = 16
PTS = 240
NX = 64
NY = 1024
N_GX = 4
N_GY = 8


phase_count = 12


upright_phase = 9


def rotor_tables():
    radius = (np.arange(BLADE_PTS) + 0.5) * ROTOR_RADIUS / BLADE_PTS
    phases = np.arange(phase_count)
    blade_ids = np.arange(BLADES)
    theta = 2.0 * np.pi * (phases[:, None] / 36.0 + blade_ids[None, :] / BLADES)
    table_y = np.floor(radius[None, None, :] * np.cos(theta)[:, :, None] + 0.5).astype(np.int32)
    table_z = np.floor(radius[None, None, :] * np.sin(theta)[:, :, None] + 0.5).astype(np.int32)
    return (table_y.reshape(phase_count, BLADES * BLADE_PTS), table_z.reshape(phase_count, BLADES * BLADE_PTS))


def turbine_layout(key):
    key = jax.random.fold_in(key, 11)
    keys = jax.random.split(key, 5)
    columns = jnp.arange(N_GX, dtype=jnp.int32)[:, None]
    members = jnp.arange(TURB_COL, dtype=jnp.int32)[None, :]
    first_one = (columns == 0) & (members == 0)
    jitter_y = jax.random.randint(keys[0], (N_GX, TURB_COL), -6, 7)
    spread_y = jax.random.randint(keys[3], (N_GX, TURB_COL), 0, NY)
    hub_y = jnp.where(first_one, jitter_y, spread_y)
    hub_x = jax.random.randint(keys[1], (N_GX, TURB_COL), 0, CX)
    hub_x = jnp.where(first_one, CX - 1, hub_x)
    hub_z = jax.random.randint(keys[4], (N_GX, TURB_COL), ROTOR_RADIUS + 1, NZ - ROTOR_RADIUS - 1)
    hub_z = jnp.where(first_one, NZ - ROTOR_RADIUS - 2, hub_z)
    phase_ids = jax.random.randint(keys[2], (N_GX, TURB_COL), 0, phase_count)
    phase_ids = jnp.where(first_one, upright_phase, phase_ids)
    table_y, table_z = rotor_tables()
    shift_y = jnp.take(jnp.asarray(table_y), phase_ids, axis=0)
    shift_z = jnp.take(jnp.asarray(table_z), phase_ids, axis=0)
    glob_y = jnp.mod(hub_y[:, :, None] + shift_y, NY).reshape(N_GX, PTS)
    levels_at = (hub_z[:, :, None] + shift_z).reshape(N_GX, PTS)
    loc_x = jnp.broadcast_to(hub_x[:, :, None], (N_GX, TURB_COL, BLADES * BLADE_PTS)).reshape(N_GX, PTS)
    owners = glob_y // CY
    loc_y = glob_y % CY
    cells = jnp.stack([loc_x, loc_y, levels_at], axis=1)
    return (owners.astype(jnp.int32), cells.astype(jnp.int32))


def draw_point_owner(key, part):
    return turbine_layout(key)[0]


def draw_point_cell(key, part):
    return turbine_layout(key)[1]


def place_value(order, position, target):
    where_now = jnp.argmax(order == target).astype(jnp.int32)
    held = order[position]
    order = order.at[where_now].set(held)
    return order.at[position].set(target)


def draw_recycle_map(key, part):
    key = jax.random.fold_in(key, 23)
    order = jax.random.permutation(key, jnp.arange(N_GY, dtype=jnp.int32))
    order = place_value(order, 0, N_GY // 2)
    order = place_value(order, 1, 2)
    return order.astype(jnp.int32)


def draw_velocity_section(key, part):
    noise = jax.random.normal(key, (3, NX, NZ, NY), jnp.float32)
    mean_flow = jnp.array([1.0, 0.0, 0.0], jnp.float32).reshape(3, 1, 1, 1)
    return mean_flow + 0.5 * noise


def steps_of(rng, extent, cuts, least, top_value):
    gain, own = 1.0, jax.random.fold_in(rng, 6)
    for axis_at, parts in cuts:
        draws = jnp.exp(jax.random.uniform(jax.random.fold_in(own, axis_at), (parts,), jnp.float32, least / len(cuts), top_value / len(cuts)))
        gain = gain * jnp.repeat(draws, extent[axis_at] // parts).reshape([-1 if axis == axis_at else 1 for axis in range(len(extent))])
    return gain


def setup_inputs(seed: int = 0) -> dict:
    arg_keys = jax.random.split(jax.random.key(seed), 6)
    velocity_section = draw_velocity_section(jax.random.fold_in(arg_keys[5], 71), 0)
    point_owner = draw_point_owner(jax.random.fold_in(arg_keys[5], 71), 0)
    point_cell = draw_point_cell(jax.random.fold_in(arg_keys[5], 71), 0)
    blade_coef = jnp.clip(jnp.exp(math.log(2.0) - 1.3862944 * jax.random.uniform(arg_keys[3], (N_GX, PTS), jnp.float32) ** steps_of(arg_keys[3], (N_GX, PTS), ((0, 4),), -0.2, 0.2)), 0.5, 2.0)
    recycle_map = draw_recycle_map(jax.random.fold_in(arg_keys[5], 71), 0)
    return dict(velocity_section=velocity_section, point_owner=point_owner, point_cell=point_cell, blade_coef=blade_coef, recycle_map=recycle_map)


viscosity = 0.02
smag_sq = 0.0256
kernel_sq = 4.0
kernel_reach = 4
force_gain = 4.0
fringe_base = 0.05
fringe_ramp = 0.45
kernel_norm = 1.0 / math.sqrt(math.pi * kernel_sq)

def kernel_weight(distance):
    inside = jnp.abs(distance) <= kernel_reach
    return jnp.where(inside, jnp.exp(-(distance * distance) / kernel_sq) * kernel_norm, 0.0).astype(jnp.float32)

def tendency(padded):
    center = padded[:, 1:-1, 1:-1, 1:-1]
    x_plus = padded[:, 2:, 1:-1, 1:-1]
    x_minus = padded[:, :-2, 1:-1, 1:-1]
    z_plus = padded[:, 1:-1, 2:, 1:-1]
    z_minus = padded[:, 1:-1, :-2, 1:-1]
    y_plus = padded[:, 1:-1, 1:-1, 2:]
    y_minus = padded[:, 1:-1, 1:-1, :-2]
    gradients = [(x_plus - x_minus) * 0.5, (y_plus - y_minus) * 0.5, (z_plus - z_minus) * 0.5]
    advect = center[0] * gradients[0] + center[1] * gradients[1] + center[2] * gradients[2]
    strain = jnp.zeros_like(center[0])
    for comp_a in range(3):
        for comp_b in range(3):
            shear = 0.5 * (gradients[comp_b][comp_a] + gradients[comp_a][comp_b])
            strain = strain + shear * shear
    eddy_visc = viscosity + smag_sq * jnp.sqrt(2.0 * strain)
    laplace = x_plus + x_minus + y_plus + y_minus + z_plus + z_minus - 6.0 * center
    return (center, eddy_visc * laplace - advect)

def point_forces(values, blade_gain):
    per_turb = BLADES * BLADE_PTS
    axial_mean = lax.optimization_barrier(jnp.mean(values[0].reshape(-1, per_turb), axis=1))
    axial_rows = jnp.repeat(axial_mean * axial_mean, per_turb)
    speeds = jnp.sqrt(lax.optimization_barrier(jnp.sum(values * values, axis=0)))
    thrust = jnp.concatenate([axial_rows[None], jnp.zeros_like(values[1:])], 0)
    return -force_gain * blade_gain[None] * (speeds[None] * values + thrust)

def reference(velocity_section, point_owner, point_cell, blade_coef, recycle_map):
    velocity = velocity_section
    source_x = 3 * N_GX // 4 * CX
    plane_rows = velocity[:, source_x]
    inflow = plane_rows.reshape(3, NZ, N_GY, CY)[:, :, recycle_map].reshape(3, NZ, NY)
    offsets = jnp.arange(-kernel_reach, kernel_reach + 1, dtype=jnp.int32)
    off_x = offsets[None, :, None, None]
    off_z = offsets[None, None, :, None]
    off_y = offsets[None, None, None, :]

    def column_step(column, carry):
        rate_all, spread_all, force_all = carry
        start = (column * CX).astype(jnp.int32)
        slab_rows = lax.dynamic_slice_in_dim(velocity, start, CX, 1)
        below = lax.dynamic_index_in_dim(velocity, jnp.maximum(start - 1, 0).astype(jnp.int32), 1, keepdims=True)
        below = jnp.where(column == 0, inflow[:, None], below)
        above = lax.dynamic_index_in_dim(velocity, jnp.minimum(start + CX, NX - 1).astype(jnp.int32), 1, keepdims=True)
        extended = jnp.concatenate([below, slab_rows, above], 1)
        extended = jnp.concatenate([extended[..., -1:], extended, extended[..., :1]], 3)
        extended = jnp.pad(extended, ((0, 0), (0, 0), (1, 1), (0, 0)))
        center, tendency_core = tendency(extended)
        x_glob = (start + jnp.arange(CX, dtype=jnp.int32)).astype(jnp.float32)
        fringe = fringe_base + fringe_ramp * (x_glob + 0.5) / NX
        tendency_core = tendency_core - fringe[None, :, None, None] * (center - inflow[:, None])
        owners = point_owner[column]
        cells = point_cell[column]
        blade_gain = blade_coef[column]
        loc_x = cells[0]
        loc_y = cells[1]
        levels_at = cells[2]
        glob_y = owners * CY + loc_y
        values = velocity[:, start + loc_x, levels_at, glob_y]
        forces = point_forces(values, blade_gain)
        idx_x = loc_x[:, None, None, None] + off_x
        idx_z = levels_at[:, None, None, None] + off_z
        idx_y = jnp.mod(glob_y[:, None, None, None] + off_y, NY)
        weight_x = jnp.where((idx_x >= 0) & (idx_x < CX), kernel_weight(off_x.astype(jnp.float32)), 0.0)
        weight_z = jnp.where((idx_z >= 0) & (idx_z < NZ), kernel_weight(off_z.astype(jnp.float32)), 0.0)
        weight_y = lax.optimization_barrier(kernel_weight(off_y.astype(jnp.float32)).astype(jnp.bfloat16)).astype(jnp.float32)
        weighted = forces[:, :, None, None, None] * weight_x[None] * weight_z[None]
        weighted = lax.optimization_barrier(weighted.astype(jnp.bfloat16)).astype(jnp.float32)
        contrib = weighted * weight_y[None]
        spread_field = jnp.zeros((3, CX, NZ, NY), jnp.float32)
        spread_field = spread_field.at[:, jnp.clip(idx_x, 0, CX - 1), jnp.clip(idx_z, 0, NZ - 1), idx_y].add(contrib)
        rate_all = lax.dynamic_update_slice_in_dim(rate_all, tendency_core, start, 1)
        spread_all = lax.dynamic_update_slice_in_dim(spread_all, spread_field, start, 1)
        force_all = lax.dynamic_update_slice_in_dim(force_all, forces[None], column.astype(jnp.int32), 0)
        return (rate_all, spread_all, force_all)
    initial = (jnp.zeros_like(velocity), jnp.zeros_like(velocity), jnp.zeros((N_GX, 3, PTS), jnp.float32))
    rate_all, spread_all, force_all = lax.fori_loop(0, N_GX, column_step, initial)
    return (rate_all, spread_all, force_all)
```

```python
import functools
import math

import jax
import jax.numpy as jnp
from jax import lax
from jax.experimental import pallas as pl
from jax.experimental.pallas import tpu as pltpu
from jax.sharding import PartitionSpec as P

BLADES = 3
BLADE_PTS = 40


viscosity = 0.02
smag_sq = 0.0256
kernel_sq = 4.0
kernel_reach = 4
force_gain = 4.0
fringe_base = 0.05
fringe_ramp = 0.45
kernel_norm = 1.0 / math.sqrt(math.pi * kernel_sq)
TILE = 8
LANES = 128
MESH = pl.DeviceIdType.MESH


def kernel_weight(distance):
    inside = jnp.abs(distance) <= kernel_reach
    return jnp.where(inside, jnp.exp(-(distance * distance) / kernel_sq) * kernel_norm, 0.0)


def exchange(
    count_x,
    count_y,
    map_ref,
    u_ref,
    owner_ref,
    cell_ref,
    below_ref,
    above_ref,
    edge_ref,
    inflow_ref,
    values_ref,
    points,
    edges,
    got_edges,
    held,
    picked,
    parts,
    x_send,
    x_recv,
    y_send,
    y_recv,
    v_send,
    v_recv,
    p1_send,
    p1_recv,
    p2_send,
    p2_recv,
    p3_send,
    p3_recv,
):
    comps, cells_x, levels, cells_y = u_ref.shape
    pts = owner_ref.shape[1]
    padded_pts = points.shape[1]
    pieces = min(count_y, levels // TILE)
    depth = levels // pieces
    gx, gy = lax.axis_index("gx"), lax.axis_index("gy")
    source = 3 * count_x // 4
    span = [lax.rem(gy + o, count_y) for o in range(count_y)]
    stream = [lax.rem(gx + o, count_x) for o in range(count_x)]
    back = [lax.rem(gy + count_y - o, count_y) for o in range(count_y)]

    def remote(src, dst, send, recv, x=None, y=None):
        return pltpu.make_async_remote_copy(
            src_ref=src,
            dst_ref=dst,
            send_sem=send,
            recv_sem=recv,
            device_id=(gx if x is None else x, gy if y is None else y),
            device_id_type=MESH,
        )

    def rows(k):
        return pl.ds(pl.multiple_of(k * depth, depth), depth)

    barrier = pltpu.get_barrier_semaphore()
    for o in range(1, count_y):
        pl.semaphore_signal(barrier, inc=1, device_id=(gx, span[o]), device_id_type=MESH)
    for o in range(1, count_x):
        pl.semaphore_signal(barrier, inc=1, device_id=(stream[o], gy), device_id_type=MESH)
    pl.semaphore_wait(barrier, count_y + count_x - 2)

    def first(o):
        return remote(
            u_ref.at[:, 0, rows(span[o])], held.at[gy], p1_send.at[o], p1_recv.at[gy], y=span[o]
        )

    @pl.when(gx == source)
    def _():
        for o in range(1, count_y):
            if pieces == count_y:
                first(o).start()
            else:
                pl.when(span[o] < pieces)(lambda o=o: first(o).start())

    up = remote(u_ref.at[:, cells_x - 1], below_ref, x_send.at[0], x_recv.at[0], x=stream[1])
    down = remote(
        u_ref.at[:, 0], above_ref, x_send.at[1], x_recv.at[1], x=stream[count_x - 1]
    )
    pl.when(gx < count_x - 1)(lambda: up.start())
    pl.when(gx > 0)(lambda: down.start())

    lane = lax.broadcasted_iota(jnp.int32, (levels, LANES), 1)
    packed = jnp.zeros((levels, LANES), jnp.float32)
    slot = lax.div(lax.rem(lane + 1, LANES), 2)
    for c in range(comps):
        for x in range(cells_x):
            n = c * cells_x + x
            packed = jnp.where(slot == n, pltpu.roll(u_ref[c, x], 2 * n, 1), packed)
    edges[...] = packed
    right = remote(edges, got_edges.at[0], y_send.at[0], y_recv.at[0], y=span[1])
    left = remote(edges, got_edges.at[1], y_send.at[1], y_recv.at[1], y=span[count_y - 1])
    right.start()
    left.start()

    def second(o):
        return remote(
            picked.at[span[o]],
            inflow_ref.at[:, rows(gy)],
            p2_send.at[o],
            p2_recv.at[gy],
            y=span[o],
        )

    def second_leg():
        held[gy] = u_ref[:, 0, rows(gy), :]
        for o in range(1, count_y):
            remote(
                held.at[back[o]], held.at[back[o]], p1_send.at[o], p1_recv.at[back[o]], y=back[o]
            ).wait_recv()
        for j in range(count_y):
            picked[j] = held[map_ref[j]]
        for o in range(1, count_y):
            second(o).start()
        inflow_ref[:, rows(gy), :] = picked[gy]

    @pl.when(gx == source)
    def _():
        if pieces == count_y:
            second_leg()
        else:
            pl.when(gy < pieces)(second_leg)

    points[...] = jnp.zeros_like(points)
    points[2:3, :] = jnp.full((1, padded_pts), -1, jnp.int32)
    points[0:1, 0:pts] = cell_ref[0, 0:1, :] * levels + cell_ref[0, 2:3, :]
    points[1:2, 0:pts] = cell_ref[0, 1:2, :]
    points[2:3, 0:pts] = owner_ref[...]

    def down_rows(row):
        spread = jnp.broadcast_to(row.astype(jnp.float32), (LANES, padded_pts))
        return spread.T

    flat = down_rows(points[0:1, :])
    at_y = down_rows(points[1:2, :])
    own = down_rows(points[2:3, :])
    lanes = lax.broadcasted_iota(jnp.int32, (padded_pts, LANES), 1).astype(jnp.float32)
    mine = (at_y == lanes) & (own == gy.astype(jnp.float32))
    chosen = jnp.concatenate(
        [
            jnp.where(flat == lanes + float(t * LANES), 1.0, 0.0).astype(jnp.bfloat16)
            for t in range(cells_x * levels // LANES)
        ],
        axis=1,
    )
    at_points = jnp.zeros((padded_pts, LANES), jnp.float32)
    for c in range(comps):
        field = u_ref[c].reshape(cells_x * levels, cells_y)
        total = jnp.zeros((padded_pts, LANES), jnp.float32)
        for _ in range(3):
            part = field.astype(jnp.bfloat16)
            total = total + jnp.dot(chosen, part, preferred_element_type=jnp.float32)
            field = field - part.astype(jnp.float32)
        column = jnp.sum(jnp.where(mine, total, 0.0), axis=1, keepdims=True)
        at_points = jnp.where(lanes == float(c), column, at_points)
    parts[gy] = at_points.T[0:TILE]

    def share(o):
        return remote(parts.at[gy], parts.at[gy], v_send.at[o], v_recv.at[gy], y=span[o])

    for o in range(1, count_y):
        share(o).start()

    def third(o, k):
        return remote(
            inflow_ref.at[:, rows(k)],
            inflow_ref.at[:, rows(k)],
            p3_send.at[o, k],
            p3_recv.at[k],
            x=stream[o],
        )

    def forward(q):
        k = lax.rem(gy + count_y - q, count_y)

        def arrived():
            remote(
                picked.at[0], inflow_ref.at[:, rows(k)], p2_send.at[0], p2_recv.at[k], y=back[1]
            ).wait_recv()

        def send_on():
            if q > 0:
                arrived()
            for o in range(1, count_x):
                third(o, k).start()

        if pieces == count_y:
            send_on()
        else:
            pl.when(k < pieces)(send_on)

    @pl.when(gx == source)
    def _():
        for q in range(count_y):
            forward(q)

    for side in range(2):
        remote(edges, got_edges.at[side], y_send.at[side], y_recv.at[side], y=span[1]).wait_recv()
    even = lax.rem(lane, 2) == 0
    edge_ref[...] = jnp.where(
        even, pltpu.roll(got_edges[0], 1, 1), pltpu.roll(got_edges[1], LANES - 1, 1)
    )

    for o in range(1, count_y):
        remote(
            parts.at[back[o]], parts.at[back[o]], v_send.at[o], v_recv.at[back[o]], y=back[o]
        ).wait_recv()
    values = parts[0]
    for j in range(1, count_y):
        values = values + parts[j]
    values_ref[...] = values

    pl.when(gx > 0)(lambda: up.wait_recv())
    pl.when(gx < count_x - 1)(lambda: down.wait_recv())

    @pl.when(gx == count_x - 1)
    def _():
        above_ref[...] = u_ref[:, cells_x - 1]

    @pl.when(gx != source)
    def _():
        for k in range(pieces):
            third(1, k).wait_recv()

    @pl.when(gx == 0)
    def _():
        below_ref[...] = inflow_ref[...]

    pl.when(gx < count_x - 1)(lambda: up.wait_send())
    pl.when(gx > 0)(lambda: down.wait_send())
    right.wait_send()
    left.wait_send()
    for o in range(1, count_y):
        share(o).wait_send()

    @pl.when(gx == source)
    def _():
        for o in range(1, count_y):
            if pieces == count_y:
                first(o).wait_send()
                second(o).wait_send()
            else:
                pl.when(span[o] < pieces)(lambda o=o: first(o).wait_send())
                pl.when(gy < pieces)(lambda o=o: second(o).wait_send())
        for o in range(1, count_x):
            for k in range(pieces):
                third(o, k).wait_send()


def compute(
    count_x,
    count_y,
    u_ref,
    below_ref,
    above_ref,
    edge_ref,
    inflow_ref,
    values_ref,
    owner_ref,
    cell_ref,
    gain_ref,
    rate_ref,
    spread_ref,
    force_ref,
    points,
    gains,
    cells,
    rate,
    spread,
    in_sem,
    rate_sem,
    spread_sem,
):
    comps, cells_x, levels, cells_y = rate.shape
    pts = owner_ref.shape[1]
    padded_pts = points.shape[1]
    per_turb = BLADES * BLADE_PTS
    gx, gy = lax.axis_index("gx"), lax.axis_index("gy")

    fetch = pltpu.make_async_copy(u_ref, cells.at[:, pl.ds(1, cells_x)], in_sem)
    fetch.start()
    cells[:, 0] = below_ref[...]
    cells[:, cells_x + 1] = above_ref[...]

    points[...] = jnp.zeros_like(points)
    gains[...] = jnp.zeros_like(gains)
    points[0:1, 0:pts] = cell_ref[0, 0:1, :]
    points[1:2, 0:pts] = owner_ref[...] * cells_y + cell_ref[0, 1:2, :]
    points[2:3, 0:pts] = cell_ref[0, 2:3, :]
    gains[0:1, 0:pts] = gain_ref[...]
    gain = gains[0:1, :]
    at = [values_ref[c : c + 1, :] for c in range(comps)]
    row = lax.broadcasted_iota(jnp.int32, (1, padded_pts), 1)
    axial = jnp.zeros((1, padded_pts), jnp.float32)
    for t in range(pts // per_turb):
        inside = (row >= t * per_turb) & (row < (t + 1) * per_turb)
        mean = jnp.sum(jnp.where(inside, at[0], 0.0), axis=1, keepdims=True) * (1.0 / per_turb)
        axial = jnp.where(inside, mean * mean, axial)
    speed = jnp.sqrt(at[0] * at[0] + at[1] * at[1] + at[2] * at[2])
    forces = []
    for c in range(comps):
        drive = speed * at[c]
        if c == 0:
            drive = drive + axial
        forces.append(-force_gain * gain * drive)
        force_ref[0, c : c + 1, :] = forces[c][:, 0:pts]

    level = lax.broadcasted_iota(jnp.int32, (levels, padded_pts), 0)
    weight_z = kernel_weight((level - points[2:3, :]).astype(jnp.float32))
    span_total = count_y * cells_y
    y_cell = lax.broadcasted_iota(jnp.int32, (cells_y, padded_pts), 0) + gy * cells_y
    distance = y_cell - points[1:2, :]
    distance = jnp.where(distance >= span_total // 2, distance - span_total, distance)
    distance = jnp.where(distance < -(span_total // 2), distance + span_total, distance)
    weight_y = kernel_weight(distance.astype(jnp.float32)).astype(jnp.bfloat16)
    point_x = points[0:1, :]

    lane = lax.broadcasted_iota(jnp.int32, (levels, cells_y), 1)
    deep = lax.broadcasted_iota(jnp.int32, (levels, cells_y), 0)
    fetch.wait()

    def plane(x):
        weight_x = kernel_weight((x - point_x).astype(jnp.float32))
        weighted = jnp.concatenate(
            [((forces[c] * weight_x) * weight_z).astype(jnp.bfloat16) for c in range(comps)], 0
        )
        spread[:, x] = lax.dot_general(
            weighted, weight_y, (((1,), (1,)), ((), ())), preferred_element_type=jnp.float32
        ).reshape(comps, levels, cells_y)
        pltpu.make_async_copy(spread.at[:, x], spread_ref.at[:, x], spread_sem.at[x]).start()

        center, grads, sums = [], [[], [], []], []
        for c in range(comps):
            here, plus, minus = cells[c, x + 1], cells[c, x + 2], cells[c, x]
            n = 2 * (c * cells_x + x)
            side = pltpu.roll(edge_ref[...], lax.rem(LANES - n, LANES), 1)
            y_minus = jnp.where(lane == 0, side, pltpu.roll(here, 1, 1))
            y_plus = jnp.where(lane == cells_y - 1, side, pltpu.roll(here, cells_y - 1, 1))
            z_minus = jnp.where(deep == 0, 0.0, pltpu.roll(here, 1, 0))
            z_plus = jnp.where(deep == levels - 1, 0.0, pltpu.roll(here, levels - 1, 0))
            center.append(here)
            grads[0].append((plus - minus) * 0.5)
            grads[1].append((y_plus - y_minus) * 0.5)
            grads[2].append((z_plus - z_minus) * 0.5)
            sums.append(plus + minus + y_plus + y_minus + z_plus + z_minus - 6.0 * here)
        diagonal = grads[0][0] * grads[0][0] + grads[1][1] * grads[1][1] + grads[2][2] * grads[2][2]
        s01 = grads[0][1] + grads[1][0]
        s02 = grads[0][2] + grads[2][0]
        s12 = grads[1][2] + grads[2][1]
        twice = 2.0 * diagonal + (s01 * s01 + s02 * s02 + s12 * s12)
        eddy = viscosity + smag_sq * jnp.sqrt(twice)
        x_glob = (gx * cells_x + x).astype(jnp.float32)
        fringe = fringe_base + fringe_ramp * (x_glob + 0.5) * (1.0 / (count_x * cells_x))
        for c in range(comps):
            advect = center[0] * grads[0][c] + center[1] * grads[1][c] + center[2] * grads[2][c]
            rate[c, x] = eddy * sums[c] - advect - fringe * (center[c] - inflow_ref[c])
        pltpu.make_async_copy(rate.at[:, x], rate_ref.at[:, x], rate_sem.at[x]).start()

    lax.fori_loop(0, cells_x, lambda x, carry: (plane(x), carry)[1], 0)

    def finish(x):
        pltpu.make_async_copy(spread.at[:, x], spread_ref.at[:, x], spread_sem.at[x]).wait()
        pltpu.make_async_copy(rate.at[:, x], rate_ref.at[:, x], rate_sem.at[x]).wait()

    lax.fori_loop(0, cells_x, lambda x, carry: (finish(x), carry)[1], 0)


def local(velocity_section, point_owner, point_cell, blade_coef, recycle_map):
    comps, cells_x, levels, cells_y = velocity_section.shape
    pts = point_owner.shape[1]
    padded_pts = -(-pts // LANES) * LANES
    count_x, count_y = lax.axis_size("gx"), lax.axis_size("gy")
    pieces = min(count_y, levels // TILE)
    depth = levels // pieces
    vmem = pl.BlockSpec(memory_space=pltpu.VMEM)
    smem = pl.BlockSpec(memory_space=pltpu.SMEM)
    hbm = pl.BlockSpec(memory_space=pl.ANY)
    f32 = jnp.float32
    plane = jax.ShapeDtypeStruct((comps, levels, cells_y), f32)
    dma = pltpu.SemaphoreType.DMA
    below, above, edge, inflow, values = pl.pallas_call(
        functools.partial(exchange, count_x, count_y),
        out_shape=(
            plane,
            plane,
            jax.ShapeDtypeStruct((levels, LANES), f32),
            plane,
            jax.ShapeDtypeStruct((TILE, padded_pts), f32),
        ),
        in_specs=[smem, vmem, vmem, vmem],
        out_specs=(vmem,) * 5,
        scratch_shapes=[
            pltpu.VMEM((TILE, padded_pts), jnp.int32),
            pltpu.VMEM((levels, LANES), f32),
            pltpu.VMEM((2, levels, LANES), f32),
            pltpu.VMEM((count_y, comps, depth, cells_y), f32),
            pltpu.VMEM((count_y, comps, depth, cells_y), f32),
            pltpu.VMEM((count_y, TILE, padded_pts), f32),
            dma((2,)),
            dma((2,)),
            dma((2,)),
            dma((2,)),
            dma((count_y,)),
            dma((count_y,)),
            dma((count_y,)),
            dma((count_y,)),
            dma((count_y,)),
            dma((count_y,)),
            dma((count_x, pieces)),
            dma((pieces,)),
        ],
        compiler_params=pltpu.CompilerParams(
            collective_id=0, has_side_effects=True, vmem_limit_bytes=32 * 1024 * 1024
        ),
        name="exchange",
    )(recycle_map, velocity_section, point_owner, point_cell)
    return pl.pallas_call(
        functools.partial(compute, count_x, count_y),
        out_shape=(
            jax.ShapeDtypeStruct(velocity_section.shape, f32),
            jax.ShapeDtypeStruct(velocity_section.shape, f32),
            jax.ShapeDtypeStruct((1, comps, pts), f32),
        ),
        in_specs=[hbm] + [vmem] * 8,
        out_specs=(hbm, hbm, vmem),
        scratch_shapes=[
            pltpu.VMEM((TILE, padded_pts), jnp.int32),
            pltpu.VMEM((TILE, padded_pts), f32),
            pltpu.VMEM((comps, cells_x + 2, levels, cells_y), f32),
            pltpu.VMEM(velocity_section.shape, f32),
            pltpu.VMEM(velocity_section.shape, f32),
            dma(()),
            dma((cells_x,)),
            dma((cells_x,)),
        ],
        compiler_params=pltpu.CompilerParams(vmem_limit_bytes=32 * 1024 * 1024),
        name="compute",
    )(
        velocity_section,
        below,
        above,
        edge,
        inflow,
        values,
        point_owner,
        point_cell,
        blade_coef,
    )


def solution(mesh):
    placed = (P(None, "gx", None, "gy"), P("gx", None), P("gx", None, None), P("gx", None), P())
    return jax.shard_map(
        local,
        mesh=mesh,
        in_specs=placed,
        out_specs=(P(None, "gx", None, "gy"), P(None, "gx", None, "gy"), P("gx", None, None)),
        check_vma=False,
    )
```

```python
import functools
import math

import jax
import jax.numpy as jnp
from jax import lax
from jax.experimental import pallas as pl
from jax.experimental.pallas import tpu as pltpu
from jax.sharding import PartitionSpec as P

BLADES = 3
BLADE_PTS = 40


viscosity = 0.02
smag_sq = 0.0256
kernel_sq = 4.0
kernel_reach = 4
force_gain = 4.0
fringe_base = 0.05
fringe_ramp = 0.45
kernel_norm = 1.0 / math.sqrt(math.pi * kernel_sq)
TILE = 8
LANES = 128
MESH = pl.DeviceIdType.MESH


def kernel_weight(distance):
    inside = jnp.abs(distance) <= kernel_reach
    return jnp.where(inside, jnp.exp(-(distance * distance) / kernel_sq) * kernel_norm, 0.0)


def evolve(
    count_x,
    count_y,
    u_ref,
    owner_ref,
    cell_ref,
    gain_ref,
    map_ref,
    core_ref,
    spread_ref,
    inflow_ref,
    force_ref,
    cells,
    owner_in,
    cell_in,
    gain_in,
    order,
    points,
    gains,
    edges,
    got_edges,
    held,
    picked,
    parts,
    in_sem,
    x_send,
    x_recv,
    y_send,
    y_recv,
    v_send,
    v_recv,
    p1_send,
    p1_recv,
    p2_send,
    p2_recv,
    p3_send,
    p3_recv,
):
    comps, cells_x, levels, cells_y = u_ref.shape
    pts = owner_ref.shape[1]
    padded_pts = points.shape[1]
    pieces = min(count_y, levels // TILE)
    depth = levels // pieces
    per_turb = BLADES * BLADE_PTS
    gx, gy = lax.axis_index("gx"), lax.axis_index("gy")
    source = 3 * count_x // 4
    span = [lax.rem(gy + o, count_y) for o in range(count_y)]
    stream = [lax.rem(gx + o, count_x) for o in range(count_x)]
    back = [lax.rem(gy + count_y - o, count_y) for o in range(count_y)]

    def remote(src, dst, send, recv, x=None, y=None):
        return pltpu.make_async_remote_copy(
            src_ref=src,
            dst_ref=dst,
            send_sem=send,
            recv_sem=recv,
            device_id=(gx if x is None else x, gy if y is None else y),
            device_id_type=MESH,
        )

    def rows(k):
        return pl.ds(pl.multiple_of(k * depth, depth), depth)

    barrier = pltpu.get_barrier_semaphore()
    for o in range(1, count_y):
        pl.semaphore_signal(barrier, inc=1, device_id=(gx, span[o]), device_id_type=MESH)
    for o in range(1, count_x):
        pl.semaphore_signal(barrier, inc=1, device_id=(stream[o], gy), device_id_type=MESH)
    fetches = [
        pltpu.make_async_copy(src, dst, in_sem.at[n])
        for n, (src, dst) in enumerate(
            [
                (u_ref, cells.at[:, pl.ds(1, cells_x)]),
                (owner_ref, owner_in),
                (cell_ref, cell_in),
                (gain_ref, gain_in),
                (map_ref, order),
            ]
        )
    ]
    for fetch in fetches:
        fetch.start()
    pl.semaphore_wait(barrier, count_y + count_x - 2)

    def first(o):
        return remote(
            u_ref.at[:, 0, rows(span[o])], held.at[gy], p1_send.at[o], p1_recv.at[gy], y=span[o]
        )

    @pl.when(gx == source)
    def _():
        for o in range(1, count_y):
            if pieces == count_y:
                first(o).start()
            else:
                pl.when(span[o] < pieces)(lambda o=o: first(o).start())

    up = remote(
        u_ref.at[:, cells_x - 1], cells.at[:, 0], x_send.at[0], x_recv.at[0], x=stream[1]
    )
    down = remote(
        u_ref.at[:, 0],
        cells.at[:, cells_x + 1],
        x_send.at[1],
        x_recv.at[1],
        x=stream[count_x - 1],
    )
    pl.when(gx < count_x - 1)(lambda: up.start())
    pl.when(gx > 0)(lambda: down.start())

    for fetch in fetches:
        fetch.wait()

    @pl.when(gx == count_x - 1)
    def _():
        cells[:, cells_x + 1] = cells[:, cells_x]

    lane = lax.broadcasted_iota(jnp.int32, (levels, LANES), 1)
    packed = jnp.zeros((levels, LANES), jnp.float32)
    slot = lax.div(lax.rem(lane + 1, LANES), 2)
    for c in range(comps):
        for x in range(cells_x):
            n = c * cells_x + x
            packed = jnp.where(slot == n, pltpu.roll(cells[c, x + 1], 2 * n, 1), packed)
    edges[...] = packed
    right = remote(edges, got_edges.at[0], y_send.at[0], y_recv.at[0], y=span[1])
    left = remote(edges, got_edges.at[1], y_send.at[1], y_recv.at[1], y=span[count_y - 1])
    right.start()
    left.start()

    def second(o):
        return remote(
            picked.at[span[o]],
            inflow_ref.at[:, rows(gy)],
            p2_send.at[o],
            p2_recv.at[gy],
            y=span[o],
        )

    def second_leg():
        held[gy] = cells[:, 1, rows(gy), :]
        for o in range(1, count_y):
            remote(
                held.at[back[o]], held.at[back[o]], p1_send.at[o], p1_recv.at[back[o]], y=back[o]
            ).wait_recv()
        for j in range(count_y):
            picked[j] = held[order[j]]
        for o in range(1, count_y):
            second(o).start()
        inflow_ref[:, rows(gy), :] = picked[gy]

    @pl.when(gx == source)
    def _():
        if pieces == count_y:
            second_leg()
        else:
            pl.when(gy < pieces)(second_leg)

    points[...] = jnp.zeros_like(points)
    gains[...] = jnp.zeros_like(gains)
    points[0:1, 0:pts] = cell_in[0] * levels + cell_in[2]
    points[1:2, 0:pts] = cell_in[1]
    points[2:3, :] = jnp.full((1, padded_pts), -1, jnp.int32)
    points[2:3, 0:pts] = owner_in[...]
    points[3:4, 0:pts] = cell_in[0]
    points[4:5, 0:pts] = owner_in[...] * cells_y + cell_in[1]
    points[5:6, 0:pts] = cell_in[2]
    gains[0:1, 0:pts] = gain_in[...]

    def down_rows(row):
        wide = jnp.broadcast_to(row.astype(jnp.float32), (LANES, padded_pts))
        return wide.T

    flat = down_rows(points[0:1, :])
    at_y = down_rows(points[1:2, :])
    own = down_rows(points[2:3, :])
    lanes = lax.broadcasted_iota(jnp.int32, (padded_pts, LANES), 1).astype(jnp.float32)
    mine = (at_y == lanes) & (own == gy.astype(jnp.float32))
    chosen = jnp.concatenate(
        [
            jnp.where(flat == lanes + float(t * LANES), 1.0, 0.0).astype(jnp.bfloat16)
            for t in range(cells_x * levels // LANES)
        ],
        axis=1,
    )
    at_points = jnp.zeros((padded_pts, LANES), jnp.float32)
    for c in range(comps):
        field = cells[c, 1 : cells_x + 1].reshape(cells_x * levels, cells_y)
        total = jnp.zeros((padded_pts, LANES), jnp.float32)
        for _ in range(3):
            part = field.astype(jnp.bfloat16)
            total = total + jnp.dot(chosen, part, preferred_element_type=jnp.float32)
            field = field - part.astype(jnp.float32)
        column = jnp.sum(jnp.where(mine, total, 0.0), axis=1, keepdims=True)
        at_points = jnp.where(lanes == float(c), column, at_points)
    parts[gy] = at_points.T[0:TILE]

    def share(o):
        return remote(parts.at[gy], parts.at[gy], v_send.at[o], v_recv.at[gy], y=span[o])

    for o in range(1, count_y):
        share(o).start()

    def third(o, k):
        return remote(
            inflow_ref.at[:, rows(k)],
            inflow_ref.at[:, rows(k)],
            p3_send.at[o, k],
            p3_recv.at[k],
            x=stream[o],
        )

    def forward(q):
        k = lax.rem(gy + count_y - q, count_y)

        def arrived():
            remote(
                picked.at[0], inflow_ref.at[:, rows(k)], p2_send.at[0], p2_recv.at[k], y=back[1]
            ).wait_recv()

        def send_on():
            if q > 0:
                arrived()
            for o in range(1, count_x):
                third(o, k).start()

        if pieces == count_y:
            send_on()
        else:
            pl.when(k < pieces)(send_on)

    @pl.when(gx == source)
    def _():
        for q in range(count_y):
            forward(q)

    for side in range(2):
        remote(edges, got_edges.at[side], y_send.at[side], y_recv.at[side], y=span[1]).wait_recv()
    right.wait_send()
    left.wait_send()
    even = lax.rem(lane, 2) == 0
    edges[...] = jnp.where(
        even, pltpu.roll(got_edges[0], 1, 1), pltpu.roll(got_edges[1], LANES - 1, 1)
    )

    deep = lax.broadcasted_iota(jnp.int32, (levels, cells_y), 0)

    def tendency(x):
        center, grads, sums = [], [[], [], []], []
        for c in range(comps):
            here, plus, minus = cells[c, x + 1], cells[c, x + 2], cells[c, x]
            n = 2 * (c * cells_x + x)
            side = pltpu.roll(edges[...], lax.rem(LANES - n, LANES), 1)
            y_minus = jnp.where(lane == 0, side, pltpu.roll(here, 1, 1))
            y_plus = jnp.where(lane == cells_y - 1, side, pltpu.roll(here, cells_y - 1, 1))
            z_minus = jnp.where(deep == 0, 0.0, pltpu.roll(here, 1, 0))
            z_plus = jnp.where(deep == levels - 1, 0.0, pltpu.roll(here, levels - 1, 0))
            center.append(here)
            grads[0].append((plus - minus) * 0.5)
            grads[1].append((y_plus - y_minus) * 0.5)
            grads[2].append((z_plus - z_minus) * 0.5)
            sums.append(plus + minus + y_plus + y_minus + z_plus + z_minus - 6.0 * here)
        diagonal = grads[0][0] * grads[0][0] + grads[1][1] * grads[1][1] + grads[2][2] * grads[2][2]
        s01 = grads[0][1] + grads[1][0]
        s02 = grads[0][2] + grads[2][0]
        s12 = grads[1][2] + grads[2][1]
        twice = 2.0 * diagonal + (s01 * s01 + s02 * s02 + s12 * s12)
        eddy = viscosity + smag_sq * jnp.sqrt(twice)
        fringe = fringe_at(gx, x, count_x, cells_x)
        for c in range(comps):
            advect = center[0] * grads[0][c] + center[1] * grads[1][c] + center[2] * grads[2][c]
            core_ref[c, x] = eddy * sums[c] - advect - fringe * center[c]

    def planes(low, high):
        lax.fori_loop(low, high, lambda x, carry: (tendency(x), carry)[1], 0)

    planes(1, cells_x - 1)

    for o in range(1, count_y):
        remote(
            parts.at[back[o]], parts.at[back[o]], v_send.at[o], v_recv.at[back[o]], y=back[o]
        ).wait_recv()
    values = parts[0]
    for j in range(1, count_y):
        values = values + parts[j]
    gain = gains[0:1, :]
    at = [values[c : c + 1] for c in range(comps)]
    row = lax.broadcasted_iota(jnp.int32, (1, padded_pts), 1)
    axial = jnp.zeros((1, padded_pts), jnp.float32)
    for t in range(pts // per_turb):
        inside = (row >= t * per_turb) & (row < (t + 1) * per_turb)
        mean = jnp.sum(jnp.where(inside, at[0], 0.0), axis=1, keepdims=True) * (1.0 / per_turb)
        axial = jnp.where(inside, mean * mean, axial)
    speed = jnp.sqrt(at[0] * at[0] + at[1] * at[1] + at[2] * at[2])
    forces = []
    for c in range(comps):
        drive = speed * at[c]
        if c == 0:
            drive = drive + axial
        forces.append(-force_gain * gain * drive)
        force_ref[c] = forces[c][:, 0:pts]

    level = lax.broadcasted_iota(jnp.int32, (levels, padded_pts), 0)
    weight_z = kernel_weight((level - points[5:6, :]).astype(jnp.float32))
    span_total = count_y * cells_y
    y_cell = lax.broadcasted_iota(jnp.int32, (cells_y, padded_pts), 0) + gy * cells_y
    distance = y_cell - points[4:5, :]
    distance = jnp.where(distance >= span_total // 2, distance - span_total, distance)
    distance = jnp.where(distance < -(span_total // 2), distance + span_total, distance)
    weight_y = kernel_weight(distance.astype(jnp.float32)).astype(jnp.bfloat16)
    point_x = points[3:4, :]

    def spread(x):
        weight_x = kernel_weight((x - point_x).astype(jnp.float32))
        weighted = jnp.concatenate(
            [((forces[c] * weight_x) * weight_z).astype(jnp.bfloat16) for c in range(comps)], 0
        )
        spread_ref[:, x] = lax.dot_general(
            weighted, weight_y, (((1,), (1,)), ((), ())), preferred_element_type=jnp.float32
        ).reshape(comps, levels, cells_y)

    lax.fori_loop(0, cells_x, lambda x, carry: (spread(x), carry)[1], 0)

    pl.when(gx > 0)(lambda: up.wait_recv())
    pl.when(gx < count_x - 1)(lambda: down.wait_recv())
    planes(cells_x - 1, cells_x)

    @pl.when(gx != source)
    def _():
        for k in range(pieces):
            third(1, k).wait_recv()

    @pl.when(gx == 0)
    def _():
        cells[:, 0] = inflow_ref[...]

    planes(0, 1)

    pl.when(gx < count_x - 1)(lambda: up.wait_send())
    pl.when(gx > 0)(lambda: down.wait_send())
    for o in range(1, count_y):
        share(o).wait_send()

    @pl.when(gx == source)
    def _():
        for o in range(1, count_y):
            if pieces == count_y:
                first(o).wait_send()
                second(o).wait_send()
            else:
                pl.when(span[o] < pieces)(lambda o=o: first(o).wait_send())
                pl.when(gy < pieces)(lambda o=o: second(o).wait_send())
        for o in range(1, count_x):
            for k in range(pieces):
                third(o, k).wait_send()


def fringe_at(gx, x, count_x, cells_x):
    x_glob = (gx * cells_x + x).astype(jnp.float32)
    return fringe_base + fringe_ramp * (x_glob + 0.5) * (1.0 / (count_x * cells_x))


def finish(
    count_x,
    core_ref,
    spread_in,
    inflow_ref,
    force_in,
    rate_ref,
    spread_ref,
    force_ref,
    rate,
    sems,
    rate_sem,
):
    comps, cells_x, levels, cells_y = rate.shape
    gx = lax.axis_index("gx")
    others = [
        pltpu.make_async_copy(spread_in, spread_ref, sems.at[0]),
        pltpu.make_async_copy(force_in, force_ref, sems.at[1]),
    ]
    for copy in others:
        copy.start()

    def out(x):
        return pltpu.make_async_copy(rate.at[:, x], rate_ref.at[:, x], rate_sem.at[x])

    for x in range(cells_x):
        fringe = fringe_at(gx, x, count_x, cells_x)
        for c in range(comps):
            rate[c, x] = core_ref[c, x] + fringe * inflow_ref[c]
        out(x).start()
    for x in range(cells_x):
        out(x).wait()
    for copy in others:
        copy.wait()


def local(velocity_section, point_owner, point_cell, blade_coef, recycle_map):
    comps, cells_x, levels, cells_y = velocity_section.shape
    pts = point_owner.shape[1]
    padded_pts = -(-pts // LANES) * LANES
    count_x, count_y = lax.axis_size("gx"), lax.axis_size("gy")
    pieces = min(count_y, levels // TILE)
    depth = levels // pieces
    vmem = pl.BlockSpec(memory_space=pltpu.VMEM)
    hbm = pl.BlockSpec(memory_space=pltpu.HBM)
    f32 = jnp.float32
    whole = jax.ShapeDtypeStruct(velocity_section.shape, f32)
    at_points = jax.ShapeDtypeStruct((comps, 1, pts), f32)
    dma = pltpu.SemaphoreType.DMA
    core, spread, inflow, force = pl.pallas_call(
        functools.partial(evolve, count_x, count_y),
        out_shape=(
            whole,
            whole,
            jax.ShapeDtypeStruct((comps, levels, cells_y), f32),
            at_points,
        ),
        in_specs=[hbm] * 5,
        out_specs=(vmem,) * 4,
        scratch_shapes=[
            pltpu.VMEM((comps, cells_x + 2, levels, cells_y), f32),
            pltpu.VMEM(point_owner.shape, jnp.int32),
            pltpu.VMEM((3, 1, pts), jnp.int32),
            pltpu.VMEM(blade_coef.shape, f32),
            pltpu.SMEM(recycle_map.shape, jnp.int32),
            pltpu.VMEM((TILE, padded_pts), jnp.int32),
            pltpu.VMEM((TILE, padded_pts), f32),
            pltpu.VMEM((levels, LANES), f32),
            pltpu.VMEM((2, levels, LANES), f32),
            pltpu.VMEM((count_y, comps, depth, cells_y), f32),
            pltpu.VMEM((count_y, comps, depth, cells_y), f32),
            pltpu.VMEM((count_y, TILE, padded_pts), f32),
            dma((5,)),
            dma((2,)),
            dma((2,)),
            dma((2,)),
            dma((2,)),
            dma((count_y,)),
            dma((count_y,)),
            dma((count_y,)),
            dma((count_y,)),
            dma((count_y,)),
            dma((count_y,)),
            dma((count_x, pieces)),
            dma((pieces,)),
        ],
        compiler_params=pltpu.CompilerParams(
            collective_id=0, has_side_effects=True, vmem_limit_bytes=32 * 1024 * 1024
        ),
        name="evolve",
    )(
        velocity_section,
        point_owner,
        point_cell.transpose(1, 0, 2),
        blade_coef,
        recycle_map,
    )
    rate, spread, force = pl.pallas_call(
        functools.partial(finish, count_x),
        out_shape=(whole, whole, at_points),
        in_specs=[vmem] * 4,
        out_specs=(hbm,) * 3,
        scratch_shapes=[
            pltpu.VMEM(velocity_section.shape, f32),
            dma((2,)),
            dma((cells_x,)),
        ],
        compiler_params=pltpu.CompilerParams(vmem_limit_bytes=16 * 1024 * 1024),
        name="finish",
    )(core, spread, inflow, force)
    return rate, spread, force.transpose(1, 0, 2)


def solution(mesh):
    placed = (P(None, "gx", None, "gy"), P("gx", None), P("gx", None, None), P("gx", None), P())
    return jax.shard_map(
        local,
        mesh=mesh,
        in_specs=placed,
        out_specs=(P(None, "gx", None, "gy"), P(None, "gx", None, "gy"), P("gx", None, None)),
        check_vma=False,
    )
```

```python
import functools
import math

import jax
import jax.numpy as jnp
from jax import lax
from jax.experimental import pallas as pl
from jax.experimental.pallas import tpu as pltpu
from jax.sharding import PartitionSpec as P

BLADES = 3
BLADE_PTS = 40


viscosity = 0.02
smag_sq = 0.0256
kernel_sq = 4.0
kernel_reach = 4
force_gain = 4.0
fringe_base = 0.05
fringe_ramp = 0.45
kernel_norm = 1.0 / math.sqrt(math.pi * kernel_sq)
TILE = 8
LANES = 128
MESH = pl.DeviceIdType.MESH


def kernel_weight(distance):
    inside = jnp.abs(distance) <= kernel_reach
    return jnp.where(inside, jnp.exp(-(distance * distance) / kernel_sq) * kernel_norm, 0.0)


def evolve(
    count_x,
    count_y,
    u_ref,
    owner_ref,
    cell_ref,
    gain_ref,
    map_ref,
    core_ref,
    spread_ref,
    inflow_ref,
    force_ref,
    cells,
    owner_in,
    cell_in,
    gain_in,
    order,
    points,
    gains,
    edges,
    got_edges,
    held,
    picked,
    parts,
    in_sem,
    x_send,
    x_recv,
    y_send,
    y_recv,
    v_send,
    v_recv,
    p1_send,
    p1_recv,
    p2_send,
    p2_recv,
):
    comps, cells_x, levels, cells_y = u_ref.shape
    pts = owner_ref.shape[1]
    padded_pts = points.shape[1]
    pieces = min(count_y, levels // TILE)
    depth = levels // pieces
    per_turb = BLADES * BLADE_PTS
    gx, gy = lax.axis_index("gx"), lax.axis_index("gy")
    source = 3 * count_x // 4
    span = [lax.rem(gy + o, count_y) for o in range(count_y)]
    stream = [lax.rem(gx + o, count_x) for o in range(count_x)]
    back = [lax.rem(gy + count_y - o, count_y) for o in range(count_y)]

    def remote(src, dst, send, recv, x=None, y=None):
        return pltpu.make_async_remote_copy(
            src_ref=src,
            dst_ref=dst,
            send_sem=send,
            recv_sem=recv,
            device_id=(gx if x is None else x, gy if y is None else y),
            device_id_type=MESH,
        )

    def rows(k):
        return pl.ds(pl.multiple_of(k * depth, depth), depth)

    barrier = pltpu.get_barrier_semaphore()

    def greet(x, y):
        pl.semaphore_signal(barrier, inc=1, device_id=(x, y), device_id_type=MESH)

    ahead = (gx < count_x - 1) & (gx + 1 != source)
    behind = (gx > 0) & (gx - 1 != source)
    for o in range(1, count_y):
        greet(gx, span[o])

    @pl.when(gx == source)
    def _():
        for x in range(1, count_x):
            for o in range(count_y):
                greet(stream[x], span[o])

    @pl.when(gx != source)
    def _():
        for o in range(count_y):
            greet(source, span[o])
        pl.when(ahead)(lambda: greet(stream[1], gy))
        pl.when(behind)(lambda: greet(stream[count_x - 1], gy))

    fetches = [
        pltpu.make_async_copy(src, dst, in_sem.at[n])
        for n, (src, dst) in enumerate(
            [
                (u_ref, cells.at[:, pl.ds(1, cells_x)]),
                (owner_ref, owner_in),
                (cell_ref, cell_in),
                (gain_ref, gain_in),
                (map_ref, order),
            ]
        )
    ]
    for fetch in fetches:
        fetch.start()

    @pl.when(gx == source)
    def _():
        pl.semaphore_wait(barrier, count_x * count_y - 1)

    @pl.when(gx != source)
    def _():
        beside = ahead.astype(jnp.int32) + behind.astype(jnp.int32)
        pl.semaphore_wait(barrier, 2 * count_y - 1 + beside)


    def first(o):
        return remote(
            u_ref.at[:, 0, rows(span[o])], held.at[gy], p1_send.at[o], p1_recv.at[gy], y=span[o]
        )

    @pl.when(gx == source)
    def _():
        for o in range(1, count_y):
            if pieces == count_y:
                first(o).start()
            else:
                pl.when(span[o] < pieces)(lambda o=o: first(o).start())

    up = remote(
        u_ref.at[:, cells_x - 1], cells.at[:, 0], x_send.at[0], x_recv.at[0], x=stream[1]
    )
    down = remote(
        u_ref.at[:, 0],
        cells.at[:, cells_x + 1],
        x_send.at[1],
        x_recv.at[1],
        x=stream[count_x - 1],
    )
    pl.when(gx < count_x - 1)(lambda: up.start())
    pl.when(gx > 0)(lambda: down.start())

    for fetch in fetches:
        fetch.wait()

    @pl.when(gx == count_x - 1)
    def _():
        cells[:, cells_x + 1] = cells[:, cells_x]

    lane = lax.broadcasted_iota(jnp.int32, (levels, LANES), 1)
    packed = jnp.zeros((levels, LANES), jnp.float32)
    slot = lax.div(lax.rem(lane + 1, LANES), 2)
    for c in range(comps):
        for x in range(cells_x):
            n = c * cells_x + x
            packed = jnp.where(slot == n, pltpu.roll(cells[c, x + 1], 2 * n, 1), packed)
    edges[...] = packed
    right = remote(edges, got_edges.at[0], y_send.at[0], y_recv.at[0], y=span[1])
    left = remote(edges, got_edges.at[1], y_send.at[1], y_recv.at[1], y=span[count_y - 1])
    right.start()
    left.start()

    def second(x, o):
        return remote(
            picked.at[span[o]],
            inflow_ref.at[:, rows(gy)],
            p2_send.at[x, o],
            p2_recv.at[gy],
            x=stream[x],
            y=span[o],
        )

    others = [(x, o) for o in range(count_y) for x in range(1, count_x)]
    others += [(0, o) for o in range(1, count_y)]

    def second_leg():
        held[gy] = cells[:, 1, rows(gy), :]
        for o in range(1, count_y):
            remote(
                held.at[back[o]], held.at[back[o]], p1_send.at[o], p1_recv.at[back[o]], y=back[o]
            ).wait_recv()
        for j in range(count_y):
            picked[j] = held[order[j]]
        for x, o in others:
            second(x, o).start()
        inflow_ref[:, rows(gy), :] = picked[gy]

    points[...] = jnp.zeros_like(points)
    gains[...] = jnp.zeros_like(gains)
    points[0:1, 0:pts] = cell_in[0] * levels + cell_in[2]
    points[1:2, 0:pts] = cell_in[1]
    points[2:3, :] = jnp.full((1, padded_pts), -1, jnp.int32)
    points[2:3, 0:pts] = owner_in[...]
    points[3:4, 0:pts] = cell_in[0]
    points[4:5, 0:pts] = owner_in[...] * cells_y + cell_in[1]
    points[5:6, 0:pts] = cell_in[2]
    gains[0:1, 0:pts] = gain_in[...]

    def down_rows(row):
        wide = jnp.broadcast_to(row.astype(jnp.float32), (LANES, padded_pts))
        return wide.T

    flat = down_rows(points[0:1, :])
    at_y = down_rows(points[1:2, :])
    own = down_rows(points[2:3, :])
    lanes = lax.broadcasted_iota(jnp.int32, (padded_pts, LANES), 1).astype(jnp.float32)
    mine = (at_y == lanes) & (own == gy.astype(jnp.float32))
    chosen = jnp.concatenate(
        [
            jnp.where(flat == lanes + float(t * LANES), 1.0, 0.0).astype(jnp.bfloat16)
            for t in range(cells_x * levels // LANES)
        ],
        axis=1,
    )
    at_points = jnp.zeros((padded_pts, LANES), jnp.float32)
    for c in range(comps):
        field = cells[c, 1 : cells_x + 1].reshape(cells_x * levels, cells_y)
        total = jnp.zeros((padded_pts, LANES), jnp.float32)
        for _ in range(3):
            part = field.astype(jnp.bfloat16)
            total = total + jnp.dot(chosen, part, preferred_element_type=jnp.float32)
            field = field - part.astype(jnp.float32)
        column = jnp.sum(jnp.where(mine, total, 0.0), axis=1, keepdims=True)
        at_points = jnp.where(lanes == float(c), column, at_points)
    parts[gy] = at_points.T[0:TILE]

    def share(o):
        return remote(parts.at[gy], parts.at[gy], v_send.at[o], v_recv.at[gy], y=span[o])

    for o in range(1, count_y):
        share(o).start()

    @pl.when(gx == source)
    def _():
        if pieces == count_y:
            second_leg()
        else:
            pl.when(gy < pieces)(second_leg)

    for side in range(2):
        remote(edges, got_edges.at[side], y_send.at[side], y_recv.at[side], y=span[1]).wait_recv()
    right.wait_send()
    left.wait_send()
    even = lax.rem(lane, 2) == 0
    edges[...] = jnp.where(
        even, pltpu.roll(got_edges[0], 1, 1), pltpu.roll(got_edges[1], LANES - 1, 1)
    )

    deep = lax.broadcasted_iota(jnp.int32, (levels, cells_y), 0)

    def tendency(x):
        center, grads, sums = [], [[], [], []], []
        for c in range(comps):
            here, plus, minus = cells[c, x + 1], cells[c, x + 2], cells[c, x]
            n = 2 * (c * cells_x + x)
            side = pltpu.roll(edges[...], lax.rem(LANES - n, LANES), 1)
            y_minus = jnp.where(lane == 0, side, pltpu.roll(here, 1, 1))
            y_plus = jnp.where(lane == cells_y - 1, side, pltpu.roll(here, cells_y - 1, 1))
            z_minus = jnp.where(deep == 0, 0.0, pltpu.roll(here, 1, 0))
            z_plus = jnp.where(deep == levels - 1, 0.0, pltpu.roll(here, levels - 1, 0))
            center.append(here)
            grads[0].append((plus - minus) * 0.5)
            grads[1].append((y_plus - y_minus) * 0.5)
            grads[2].append((z_plus - z_minus) * 0.5)
            sums.append(plus + minus + y_plus + y_minus + z_plus + z_minus - 6.0 * here)
        diagonal = grads[0][0] * grads[0][0] + grads[1][1] * grads[1][1] + grads[2][2] * grads[2][2]
        s01 = grads[0][1] + grads[1][0]
        s02 = grads[0][2] + grads[2][0]
        s12 = grads[1][2] + grads[2][1]
        twice = 2.0 * diagonal + (s01 * s01 + s02 * s02 + s12 * s12)
        eddy = viscosity + smag_sq * jnp.sqrt(twice)
        fringe = fringe_at(gx, x, count_x, cells_x)
        for c in range(comps):
            advect = center[0] * grads[0][c] + center[1] * grads[1][c] + center[2] * grads[2][c]
            core_ref[c, x] = eddy * sums[c] - advect - fringe * center[c]

    def planes(low, high):
        lax.fori_loop(low, high, lambda x, carry: (tendency(x), carry)[1], 0)

    planes(1, cells_x - 1)

    for o in range(1, count_y):
        remote(
            parts.at[back[o]], parts.at[back[o]], v_send.at[o], v_recv.at[back[o]], y=back[o]
        ).wait_recv()
    values = parts[0]
    for j in range(1, count_y):
        values = values + parts[j]
    gain = gains[0:1, :]
    at = [values[c : c + 1] for c in range(comps)]
    row = lax.broadcasted_iota(jnp.int32, (1, padded_pts), 1)
    axial = jnp.zeros((1, padded_pts), jnp.float32)
    for t in range(pts // per_turb):
        inside = (row >= t * per_turb) & (row < (t + 1) * per_turb)
        mean = jnp.sum(jnp.where(inside, at[0], 0.0), axis=1, keepdims=True) * (1.0 / per_turb)
        axial = jnp.where(inside, mean * mean, axial)
    speed = jnp.sqrt(at[0] * at[0] + at[1] * at[1] + at[2] * at[2])
    forces = []
    for c in range(comps):
        drive = speed * at[c]
        if c == 0:
            drive = drive + axial
        forces.append(-force_gain * gain * drive)
        force_ref[c] = forces[c][:, 0:pts]

    level = lax.broadcasted_iota(jnp.int32, (levels, padded_pts), 0)
    weight_z = kernel_weight((level - points[5:6, :]).astype(jnp.float32))
    span_total = count_y * cells_y
    y_cell = lax.broadcasted_iota(jnp.int32, (cells_y, padded_pts), 0) + gy * cells_y
    distance = y_cell - points[4:5, :]
    distance = jnp.where(distance >= span_total // 2, distance - span_total, distance)
    distance = jnp.where(distance < -(span_total // 2), distance + span_total, distance)
    weight_y = kernel_weight(distance.astype(jnp.float32)).astype(jnp.bfloat16)
    point_x = points[3:4, :]

    group = 4

    def spread(step):
        weighted = []
        for x in range(group):
            weight_x = kernel_weight((step * group + x - point_x).astype(jnp.float32))
            for c in range(comps):
                weighted.append(((forces[c] * weight_x) * weight_z).astype(jnp.bfloat16))
        summed = lax.dot_general(
            jnp.concatenate(weighted, 0),
            weight_y,
            (((1,), (1,)), ((), ())),
            preferred_element_type=jnp.float32,
        ).reshape(group, comps, levels, cells_y)
        for x in range(group):
            spread_ref[:, step * group + x] = summed[x]

    lax.fori_loop(0, cells_x // group, lambda x, carry: (spread(x), carry)[1], 0)

    pl.when(gx > 0)(lambda: up.wait_recv())
    pl.when(gx < count_x - 1)(lambda: down.wait_recv())
    planes(cells_x - 1, cells_x)

    for k in range(pieces):
        landing = inflow_ref.at[:, pl.ds(k * depth, depth)]

        @pl.when((gx != source) | (gy != k))
        def _(k=k, landing=landing):
            remote(picked.at[0], landing, p2_send.at[0, 0], p2_recv.at[k], y=back[1]).wait_recv()

    @pl.when(gx == 0)
    def _():
        cells[:, 0] = inflow_ref[...]

    planes(0, 1)

    pl.when(gx < count_x - 1)(lambda: up.wait_send())
    pl.when(gx > 0)(lambda: down.wait_send())
    for o in range(1, count_y):
        share(o).wait_send()

    @pl.when(gx == source)
    def _():
        for o in range(1, count_y):
            if pieces == count_y:
                first(o).wait_send()
            else:
                pl.when(span[o] < pieces)(lambda o=o: first(o).wait_send())
        for x, o in others:
            if pieces == count_y:
                second(x, o).wait_send()
            else:
                pl.when(gy < pieces)(lambda x=x, o=o: second(x, o).wait_send())


def fringe_at(gx, x, count_x, cells_x):
    x_glob = (gx * cells_x + x).astype(jnp.float32)
    return fringe_base + fringe_ramp * (x_glob + 0.5) * (1.0 / (count_x * cells_x))


def finish(
    count_x,
    core_ref,
    spread_in,
    inflow_ref,
    force_in,
    rate_ref,
    spread_ref,
    force_ref,
    rate,
    sems,
    rate_sem,
):
    comps, cells_x, levels, cells_y = rate.shape
    gx = lax.axis_index("gx")
    others = [
        pltpu.make_async_copy(spread_in, spread_ref, sems.at[0]),
        pltpu.make_async_copy(force_in, force_ref, sems.at[1]),
    ]
    for copy in others:
        copy.start()

    def out(x):
        return pltpu.make_async_copy(rate.at[:, x], rate_ref.at[:, x], rate_sem.at[x])

    for x in range(cells_x):
        fringe = fringe_at(gx, x, count_x, cells_x)
        for c in range(comps):
            rate[c, x] = core_ref[c, x] + fringe * inflow_ref[c]
        out(x).start()
    for x in range(cells_x):
        out(x).wait()
    for copy in others:
        copy.wait()


def local(velocity_section, point_owner, point_cell, blade_coef, recycle_map):
    comps, cells_x, levels, cells_y = velocity_section.shape
    pts = point_owner.shape[1]
    padded_pts = -(-pts // LANES) * LANES
    count_x, count_y = lax.axis_size("gx"), lax.axis_size("gy")
    pieces = min(count_y, levels // TILE)
    depth = levels // pieces
    vmem = pl.BlockSpec(memory_space=pltpu.VMEM)
    hbm = pl.BlockSpec(memory_space=pltpu.HBM)
    f32 = jnp.float32
    whole = jax.ShapeDtypeStruct(velocity_section.shape, f32)
    at_points = jax.ShapeDtypeStruct((comps, 1, pts), f32)
    dma = pltpu.SemaphoreType.DMA
    core, spread, inflow, force = pl.pallas_call(
        functools.partial(evolve, count_x, count_y),
        out_shape=(
            whole,
            whole,
            jax.ShapeDtypeStruct((comps, levels, cells_y), f32),
            at_points,
        ),
        in_specs=[hbm] * 5,
        out_specs=(vmem,) * 4,
        scratch_shapes=[
            pltpu.VMEM((comps, cells_x + 2, levels, cells_y), f32),
            pltpu.VMEM(point_owner.shape, jnp.int32),
            pltpu.VMEM((3, 1, pts), jnp.int32),
            pltpu.VMEM(blade_coef.shape, f32),
            pltpu.SMEM(recycle_map.shape, jnp.int32),
            pltpu.VMEM((TILE, padded_pts), jnp.int32),
            pltpu.VMEM((TILE, padded_pts), f32),
            pltpu.VMEM((levels, LANES), f32),
            pltpu.VMEM((2, levels, LANES), f32),
            pltpu.VMEM((count_y, comps, depth, cells_y), f32),
            pltpu.VMEM((count_y, comps, depth, cells_y), f32),
            pltpu.VMEM((count_y, TILE, padded_pts), f32),
            dma((5,)),
            dma((2,)),
            dma((2,)),
            dma((2,)),
            dma((2,)),
            dma((count_y,)),
            dma((count_y,)),
            dma((count_y,)),
            dma((count_y,)),
            dma((count_x, count_y)),
            dma((pieces,)),
        ],
        compiler_params=pltpu.CompilerParams(
            collective_id=0, has_side_effects=True, vmem_limit_bytes=32 * 1024 * 1024
        ),
        name="evolve",
    )(
        *(
            pltpu.with_memory_space_constraint(operand, pltpu.HBM)
            for operand in (
                velocity_section,
                point_owner,
                point_cell.transpose(1, 0, 2),
                blade_coef,
                recycle_map,
            )
        )
    )
    rate, spread, force = pl.pallas_call(
        functools.partial(finish, count_x),
        out_shape=(whole, whole, at_points),
        in_specs=[vmem] * 4,
        out_specs=(hbm,) * 3,
        scratch_shapes=[
            pltpu.VMEM(velocity_section.shape, f32),
            dma((2,)),
            dma((cells_x,)),
        ],
        compiler_params=pltpu.CompilerParams(vmem_limit_bytes=16 * 1024 * 1024),
        name="finish",
    )(core, spread, inflow, force)
    return rate, spread, force.transpose(1, 0, 2)


def solution(mesh):
    placed = (P(None, "gx", None, "gy"), P("gx", None), P("gx", None, None), P("gx", None), P())
    return jax.shard_map(
        local,
        mesh=mesh,
        in_specs=placed,
        out_specs=(P(None, "gx", None, "gy"), P(None, "gx", None, "gy"), P("gx", None, None)),
        check_vma=False,
    )
```

```python
import functools
import math

import jax
import jax.numpy as jnp
from jax import lax
from jax.experimental import pallas as pl
from jax.experimental.pallas import tpu as pltpu
from jax.sharding import PartitionSpec as P

BLADES = 3
BLADE_PTS = 40


viscosity = 0.02
smag_sq = 0.0256
kernel_sq = 4.0
kernel_reach = 4
force_gain = 4.0
fringe_base = 0.05
fringe_ramp = 0.45
kernel_norm = 1.0 / math.sqrt(math.pi * kernel_sq)
TILE = 8
LANES = 128
MESH = pl.DeviceIdType.MESH


def kernel_weight(distance):
    inside = jnp.abs(distance) <= kernel_reach
    return jnp.where(inside, jnp.exp(-(distance * distance) / kernel_sq) * kernel_norm, 0.0)


def evolve(
    count_x,
    count_y,
    u_ref,
    owner_ref,
    cell_ref,
    gain_ref,
    map_ref,
    core_ref,
    spread_ref,
    inflow_ref,
    force_ref,
    cells,
    owner_in,
    cell_in,
    gain_in,
    order,
    points,
    gains,
    near_x,
    near_y,
    near_z,
    edges,
    sides,
    got_edges,
    held,
    picked,
    parts,
    in_sem,
    x_send,
    x_recv,
    y_send,
    y_recv,
    v_send,
    v_recv,
    p1_send,
    p1_recv,
    p2_send,
    p2_recv,
):
    comps, cells_x, levels, cells_y = u_ref.shape
    pts = owner_ref.shape[1]
    padded_pts = points.shape[1]
    pieces = min(count_y, levels // TILE)
    depth = levels // pieces
    per_turb = BLADES * BLADE_PTS
    gx, gy = lax.axis_index("gx"), lax.axis_index("gy")
    source = 3 * count_x // 4
    span = [lax.rem(gy + o, count_y) for o in range(count_y)]
    stream = [lax.rem(gx + o, count_x) for o in range(count_x)]
    back = [lax.rem(gy + count_y - o, count_y) for o in range(count_y)]

    def remote(src, dst, send, recv, x=None, y=None):
        return pltpu.make_async_remote_copy(
            src_ref=src,
            dst_ref=dst,
            send_sem=send,
            recv_sem=recv,
            device_id=(gx if x is None else x, gy if y is None else y),
            device_id_type=MESH,
        )

    def rows(k):
        return pl.ds(pl.multiple_of(k * depth, depth), depth)

    def inner_rows(k):
        return pl.ds(pl.multiple_of(k * depth, depth) + TILE, depth)

    barrier = pltpu.get_barrier_semaphore()

    def greet(x, y):
        pl.semaphore_signal(barrier, inc=1, device_id=(x, y), device_id_type=MESH)

    ahead = (gx < count_x - 1) & (gx + 1 != source)
    behind = (gx > 0) & (gx - 1 != source)
    for o in range(1, count_y):
        greet(gx, span[o])

    @pl.when(gx == source)
    def _():
        for x in range(1, count_x):
            for o in range(count_y):
                greet(stream[x], span[o])

    @pl.when(gx != source)
    def _():
        for o in range(count_y):
            greet(source, span[o])
        pl.when(ahead)(lambda: greet(stream[1], gy))
        pl.when(behind)(lambda: greet(stream[count_x - 1], gy))

    inner = pl.ds(TILE, levels)
    fetches = [
        pltpu.make_async_copy(src, dst, in_sem.at[n])
        for n, (src, dst) in enumerate(
            [
                (u_ref, cells.at[:, pl.ds(1, cells_x), inner]),
                (owner_ref, owner_in),
                (cell_ref, cell_in),
                (gain_ref, gain_in),
                (map_ref, order),
            ]
        )
    ]
    for fetch in fetches:
        fetch.start()

    @pl.when(gx == source)
    def _():
        pl.semaphore_wait(barrier, count_x * count_y - 1)

    @pl.when(gx != source)
    def _():
        beside = ahead.astype(jnp.int32) + behind.astype(jnp.int32)
        pl.semaphore_wait(barrier, 2 * count_y - 1 + beside)


    for fetch in fetches:
        fetch.wait()

    def first(o):
        return remote(
            cells.at[:, 1, inner_rows(span[o])], held.at[gy], p1_send.at[o], p1_recv.at[gy], y=span[o]
        )

    @pl.when(gx == source)
    def _():
        for o in range(1, count_y):
            if pieces == count_y:
                first(o).start()
            else:
                pl.when(span[o] < pieces)(lambda o=o: first(o).start())

    up = remote(
        u_ref.at[:, cells_x - 1], cells.at[:, 0, inner], x_send.at[0], x_recv.at[0], x=stream[1]
    )
    down = remote(
        u_ref.at[:, 0],
        cells.at[:, cells_x + 1, inner],
        x_send.at[1],
        x_recv.at[1],
        x=stream[count_x - 1],
    )
    pl.when(gx < count_x - 1)(lambda: up.start())
    pl.when(gx > 0)(lambda: down.start())

    @pl.when(gx == count_x - 1)
    def _():
        cells[:, cells_x + 1, inner] = cells[:, cells_x, inner]

    cells[:, :, 0:TILE] = jnp.zeros((comps, cells_x + 2, TILE, cells_y), jnp.float32)
    cells[:, :, TILE + levels :] = jnp.zeros((comps, cells_x + 2, TILE, cells_y), jnp.float32)

    lane = lax.broadcasted_iota(jnp.int32, (levels, LANES), 1)
    packed = jnp.zeros((levels, LANES), jnp.float32)
    slot = lax.div(lax.rem(lane + 1, LANES), 2)
    for c in range(comps):
        for x in range(cells_x):
            n = c * cells_x + x
            packed = jnp.where(slot == n, pltpu.roll(cells[c, x + 1, inner], 2 * n, 1), packed)
    even = lax.rem(lane, 2) == 0
    upper, lower = packed[0 : levels // 2], packed[levels // 2 :]
    even_half = even[0 : levels // 2]
    sides[0] = jnp.where(even_half, pltpu.roll(lower, 1, 1), upper)
    sides[1] = jnp.where(even_half, upper, pltpu.roll(lower, LANES - 1, 1))
    right = remote(sides.at[0], got_edges.at[0], y_send.at[0], y_recv.at[0], y=span[1])
    left = remote(
        sides.at[1], got_edges.at[1], y_send.at[1], y_recv.at[1], y=span[count_y - 1]
    )
    right.start()
    left.start()

    def second(x, o):
        return remote(
            picked.at[span[o]],
            inflow_ref.at[:, rows(gy)],
            p2_send.at[x, o],
            p2_recv.at[gy],
            x=stream[x],
            y=span[o],
        )

    others = [(x, o) for o in range(count_y) for x in range(1, count_x)]
    others += [(0, o) for o in range(1, count_y)]

    def second_leg():
        held[gy] = cells[:, 1, pl.ds(pl.multiple_of(gy * depth, depth) + TILE, depth), :]
        for o in range(1, count_y):
            remote(
                held.at[back[o]], held.at[back[o]], p1_send.at[o], p1_recv.at[back[o]], y=back[o]
            ).wait_recv()
        for j in range(count_y):
            picked[j] = held[order[j]]
        for x, o in others:
            second(x, o).start()
        inflow_ref[:, rows(gy), :] = picked[gy]

    points[...] = jnp.zeros_like(points)
    gains[...] = jnp.zeros_like(gains)
    points[0:1, 0:pts] = cell_in[0] * levels + cell_in[2]
    points[1:2, 0:pts] = cell_in[1]
    points[2:3, :] = jnp.full((1, padded_pts), -1, jnp.int32)
    points[2:3, 0:pts] = owner_in[...]
    points[3:4, 0:pts] = cell_in[0]
    points[4:5, 0:pts] = owner_in[...] * cells_y + cell_in[1]
    points[5:6, 0:pts] = cell_in[2]
    gains[0:1, 0:pts] = gain_in[...]

    def down_rows(row):
        wide = jnp.broadcast_to(row.astype(jnp.float32), (LANES, padded_pts))
        return wide.T

    flat = down_rows(points[0:1, :])
    at_y = down_rows(points[1:2, :])
    own = down_rows(points[2:3, :])
    lanes = lax.broadcasted_iota(jnp.int32, (padded_pts, LANES), 1).astype(jnp.float32)
    mine = (at_y == lanes) & (own == gy.astype(jnp.float32))
    chosen = jnp.concatenate(
        [
            jnp.where(flat == lanes + float(t * LANES), 1.0, 0.0).astype(jnp.bfloat16)
            for t in range(cells_x * levels // LANES)
        ],
        axis=1,
    )
    at_points = jnp.zeros((padded_pts, LANES), jnp.float32)
    point = lax.broadcasted_iota(jnp.int32, (padded_pts, LANES), 0)
    part_row = (lax.div(point, LANES) * comps).astype(jnp.float32)
    for c in range(comps):
        field = cells[c, 1 : cells_x + 1, TILE : TILE + levels].reshape(cells_x * levels, cells_y)
        total = jnp.zeros((padded_pts, LANES), jnp.float32)
        for _ in range(3):
            part = field.astype(jnp.bfloat16)
            total = total + jnp.dot(chosen, part, preferred_element_type=jnp.float32)
            field = field - part.astype(jnp.float32)
        column = jnp.sum(jnp.where(mine, total, 0.0), axis=1, keepdims=True)
        at_points = jnp.where(lanes == part_row + float(c), column, at_points)
    folded = at_points[0:LANES]
    for h in range(1, padded_pts // LANES):
        folded = folded + at_points[h * LANES : (h + 1) * LANES]
    parts[gy] = folded.T[0:TILE]

    def share(o):
        return remote(parts.at[gy], parts.at[gy], v_send.at[o], v_recv.at[gy], y=span[o])

    for o in range(1, count_y):
        share(o).start()

    @pl.when(gx == source)
    def _():
        if pieces == count_y:
            second_leg()
        else:
            pl.when(gy < pieces)(second_leg)

    deep = lax.broadcasted_iota(jnp.int32, (cells_x, padded_pts), 0)
    near_x[...] = kernel_weight((deep - points[3:4, :]).astype(jnp.float32))
    level = lax.broadcasted_iota(jnp.int32, (levels, padded_pts), 0)
    near_z[...] = kernel_weight((level - points[5:6, :]).astype(jnp.float32))
    span_total = count_y * cells_y
    y_cell = lax.broadcasted_iota(jnp.int32, (cells_y, padded_pts), 0) + gy * cells_y
    distance = y_cell - points[4:5, :]
    distance = jnp.where(distance >= span_total // 2, distance - span_total, distance)
    distance = jnp.where(distance < -(span_total // 2), distance + span_total, distance)
    near_y[...] = kernel_weight(distance.astype(jnp.float32)).astype(jnp.bfloat16)

    for side in range(2):
        remote(
            sides.at[side], got_edges.at[side], y_send.at[side], y_recv.at[side], y=span[1]
        ).wait_recv()
    from_left, from_right = got_edges[0], got_edges[1]
    edges[0 : levels // 2] = jnp.where(
        even_half, pltpu.roll(from_left, 1, 1), pltpu.roll(from_right, LANES - 1, 1)
    )
    edges[levels // 2 :] = jnp.where(even_half, from_left, from_right)

    def tendency(x):
        half, grads, sums, drag = [], [[], [], []], [], []
        fringe = fringe_at(gx, x, count_x, cells_x)
        for c in range(comps):
            here = cells[c, x + 1, inner]
            plus, minus = cells[c, x + 2, inner], cells[c, x, inner]
            z_plus = cells[c, x + 1, TILE + 1 : TILE + 1 + levels]
            z_minus = cells[c, x + 1, TILE - 1 : TILE - 1 + levels]
            n = 2 * (c * cells_x + x)
            side = pltpu.roll(edges[...], lax.rem(LANES - n, LANES), 1)
            y_minus = jnp.where(lane == 0, side, pltpu.roll(here, 1, 1))
            y_plus = jnp.where(lane == cells_y - 1, side, pltpu.roll(here, cells_y - 1, 1))
            half.append(0.5 * here)
            grads[0].append(plus - minus)
            grads[1].append(y_plus - y_minus)
            grads[2].append(z_plus - z_minus)
            sums.append((plus + minus) + (y_plus + y_minus) + (z_plus + z_minus) - 6.0 * here)
            drag.append(fringe * here)
        diagonal = grads[0][0] * grads[0][0] + grads[1][1] * grads[1][1] + grads[2][2] * grads[2][2]
        s01 = grads[0][1] + grads[1][0]
        s02 = grads[0][2] + grads[2][0]
        s12 = grads[1][2] + grads[2][1]
        twice = (diagonal + diagonal) + (s01 * s01 + s02 * s02 + s12 * s12)
        eddy = viscosity + (0.5 * smag_sq) * jnp.sqrt(twice)
        for c in range(comps):
            advect = half[0] * grads[0][c] + half[1] * grads[1][c] + half[2] * grads[2][c]
            core_ref[c, x] = eddy * sums[c] - (advect + drag[c])

    def planes(low, high):
        lax.fori_loop(low, high, lambda x, carry: (tendency(x), carry)[1], 0)

    early = cells_x // 2 - 1
    planes(1, early)

    for o in range(1, count_y):
        remote(
            parts.at[back[o]], parts.at[back[o]], v_send.at[o], v_recv.at[back[o]], y=back[o]
        ).wait_recv()
    values = parts[0]
    for j in range(1, count_y):
        values = values + parts[j]
    gain = gains[0:1, :]
    at = [
        jnp.concatenate(
            [values[h * comps + c : h * comps + c + 1] for h in range(padded_pts // LANES)], 1
        )
        for c in range(comps)
    ]
    row = lax.broadcasted_iota(jnp.int32, (1, padded_pts), 1)
    axial = jnp.zeros((1, padded_pts), jnp.float32)
    for t in range(pts // per_turb):
        inside = (row >= t * per_turb) & (row < (t + 1) * per_turb)
        mean = jnp.sum(jnp.where(inside, at[0], 0.0), axis=1, keepdims=True) * (1.0 / per_turb)
        axial = jnp.where(inside, mean * mean, axial)
    speed = jnp.sqrt(at[0] * at[0] + at[1] * at[1] + at[2] * at[2])
    forces = []
    for c in range(comps):
        drive = speed * at[c]
        if c == 0:
            drive = drive + axial
        forces.append(-force_gain * gain * drive)
        force_ref[c] = forces[c][:, 0:pts]

    group = 2

    def spread(step):
        weighted = []
        for x in range(group):
            weight_x = near_x[pl.ds(step * group + x, 1), :]
            for c in range(comps):
                weighted.append(((forces[c] * weight_x) * near_z[...]).astype(jnp.bfloat16))
        summed = lax.dot_general(
            jnp.concatenate(weighted, 0),
            near_y[...],
            (((1,), (1,)), ((), ())),
            preferred_element_type=jnp.float32,
        ).reshape(group, comps, levels, cells_y)
        for x in range(group):
            spread_ref[:, step * group + x] = summed[x]

    def both(step, carry):
        spread(step)
        tendency(early + step)
        return carry

    lax.fori_loop(0, cells_x // group, both, 0)

    pl.when(gx > 0)(lambda: up.wait_recv())
    pl.when(gx < count_x - 1)(lambda: down.wait_recv())
    planes(cells_x - 1, cells_x)

    for k in range(pieces):
        landing = inflow_ref.at[:, pl.ds(k * depth, depth)]

        @pl.when((gx != source) | (gy != k))
        def _(k=k, landing=landing):
            remote(picked.at[0], landing, p2_send.at[0, 0], p2_recv.at[k], y=back[1]).wait_recv()

    @pl.when(gx == 0)
    def _():
        cells[:, 0, inner] = inflow_ref[...]

    planes(0, 1)

    right.wait_send()
    left.wait_send()
    pl.when(gx < count_x - 1)(lambda: up.wait_send())
    pl.when(gx > 0)(lambda: down.wait_send())
    for o in range(1, count_y):
        share(o).wait_send()

    @pl.when(gx == source)
    def _():
        for o in range(1, count_y):
            if pieces == count_y:
                first(o).wait_send()
            else:
                pl.when(span[o] < pieces)(lambda o=o: first(o).wait_send())
        for x, o in others:
            if pieces == count_y:
                second(x, o).wait_send()
            else:
                pl.when(gy < pieces)(lambda x=x, o=o: second(x, o).wait_send())


def fringe_at(gx, x, count_x, cells_x):
    x_glob = (gx * cells_x + x).astype(jnp.float32)
    return fringe_base + fringe_ramp * (x_glob + 0.5) * (1.0 / (count_x * cells_x))


def finish(
    count_x,
    core_ref,
    spread_in,
    inflow_ref,
    force_in,
    rate_ref,
    spread_ref,
    force_ref,
    rate,
    sems,
    rate_sem,
):
    comps, cells_x, levels, cells_y = rate.shape
    gx = lax.axis_index("gx")
    others = [
        pltpu.make_async_copy(spread_in.at[c], spread_ref.at[c], sems.at[c + 1])
        for c in range(comps)
    ]
    others.append(pltpu.make_async_copy(force_in, force_ref, sems.at[0]))
    for copy in others:
        copy.start()

    def out(c):
        return pltpu.make_async_copy(rate.at[c], rate_ref.at[c], rate_sem.at[c])

    for c in range(comps):
        for x in range(cells_x):
            rate[c, x] = core_ref[c, x] + fringe_at(gx, x, count_x, cells_x) * inflow_ref[c]
        out(c).start()
    for c in range(comps):
        out(c).wait()
    for copy in others:
        copy.wait()


def local(velocity_section, point_owner, point_cell, blade_coef, recycle_map):
    comps, cells_x, levels, cells_y = velocity_section.shape
    pts = point_owner.shape[1]
    padded_pts = -(-pts // LANES) * LANES
    count_x, count_y = lax.axis_size("gx"), lax.axis_size("gy")
    pieces = min(count_y, levels // TILE)
    depth = levels // pieces
    vmem = pl.BlockSpec(memory_space=pltpu.VMEM)
    hbm = pl.BlockSpec(memory_space=pltpu.HBM)
    f32 = jnp.float32
    whole = jax.ShapeDtypeStruct(velocity_section.shape, f32)
    at_points = jax.ShapeDtypeStruct((comps, 1, pts), f32)
    dma = pltpu.SemaphoreType.DMA
    core, spread, inflow, force = pl.pallas_call(
        functools.partial(evolve, count_x, count_y),
        out_shape=(
            whole,
            whole,
            jax.ShapeDtypeStruct((comps, levels, cells_y), f32),
            at_points,
        ),
        in_specs=[hbm] * 5,
        out_specs=(vmem,) * 4,
        scratch_shapes=[
            pltpu.VMEM((comps, cells_x + 2, levels + 2 * TILE, cells_y), f32),
            pltpu.VMEM(point_owner.shape, jnp.int32),
            pltpu.VMEM((3, 1, pts), jnp.int32),
            pltpu.VMEM(blade_coef.shape, f32),
            pltpu.SMEM(recycle_map.shape, jnp.int32),
            pltpu.VMEM((TILE, padded_pts), jnp.int32),
            pltpu.VMEM((TILE, padded_pts), f32),
            pltpu.VMEM((cells_x, padded_pts), f32),
            pltpu.VMEM((cells_y, padded_pts), jnp.bfloat16),
            pltpu.VMEM((levels, padded_pts), f32),
            pltpu.VMEM((levels, LANES), f32),
            pltpu.VMEM((2, levels // 2, LANES), f32),
            pltpu.VMEM((2, levels // 2, LANES), f32),
            pltpu.VMEM((count_y, comps, depth, cells_y), f32),
            pltpu.VMEM((count_y, comps, depth, cells_y), f32),
            pltpu.VMEM((count_y, TILE, LANES), f32),
            dma((5,)),
            dma((2,)),
            dma((2,)),
            dma((2,)),
            dma((2,)),
            dma((count_y,)),
            dma((count_y,)),
            dma((count_y,)),
            dma((count_y,)),
            dma((count_x, count_y)),
            dma((pieces,)),
        ],
        compiler_params=pltpu.CompilerParams(
            collective_id=0, has_side_effects=True, vmem_limit_bytes=32 * 1024 * 1024
        ),
        name="evolve",
    )(
        *(
            pltpu.with_memory_space_constraint(operand, pltpu.HBM)
            for operand in (
                velocity_section,
                point_owner,
                point_cell.transpose(1, 0, 2),
                blade_coef,
                recycle_map,
            )
        )
    )
    rate, spread, force = pl.pallas_call(
        functools.partial(finish, count_x),
        out_shape=(whole, whole, at_points),
        in_specs=[vmem] * 4,
        out_specs=(hbm,) * 3,
        scratch_shapes=[
            pltpu.VMEM(velocity_section.shape, f32),
            dma((comps + 1,)),
            dma((comps,)),
        ],
        compiler_params=pltpu.CompilerParams(vmem_limit_bytes=16 * 1024 * 1024),
        name="finish",
    )(core, spread, inflow, force)
    return rate, spread, force.transpose(1, 0, 2)


def solution(mesh):
    placed = (P(None, "gx", None, "gy"), P("gx", None), P("gx", None, None), P("gx", None), P())
    return jax.shard_map(
        local,
        mesh=mesh,
        in_specs=placed,
        out_specs=(P(None, "gx", None, "gy"), P(None, "gx", None, "gy"), P("gx", None, None)),
        check_vma=False,
    )
```
